256 devices in a mesh: gx: 16 (over x, y_lo, core), gy: 16 (over z, y_hi).
Axes of the slice: x: 4, y: 4 (y_hi: 2, y_lo: 2; y = y_hi * 2 + y_lo), z: 8, core: 2. Of those that a mesh axis runs over, the one named last changes fastest.
Arguments:
- tokens: bfloat16 [512, 16384], P('gy', 'gx'), may hold values from -6 to 6
- gate_weight: bfloat16 [16384, 26624], P('gx', 'gy'), may hold values from -0.046875 to 0.046875
- up_weight: bfloat16 [16384, 26624], P('gx', 'gy'), may hold values from -0.046875 to 0.046875
- down_weight: bfloat16 [26624, 16384], P('gy', 'gx'), may hold values from -0.0390625 to 0.0390625
Outputs:
- block_out: bfloat16 [512, 16384], P('gy', 'gx')
The draws below stay inside these ranges and needn't reach their ends.
All inputs are finite; a program needn't handle non-finite values.
Results may differ from the reference program's by a relative error of at most 0.0039.
Values may be sent and summed in bfloat16 or wider, within the bound.
A program may use at most 64 MiB of HBM per device.

```python
import jax
import jax.numpy as jnp

D = 16384
FF = 26624
TOKENS = 512


def draw_tokens(key, part):
    key = jax.random.fold_in(key, 11)
    values = jnp.clip(jax.random.normal(key, (TOKENS, D), jnp.float32), -6.0, 6.0)
    return values.astype(jnp.bfloat16)


def steps_of(stream_key, extent, pieces, low, top_value):
    gain = 1.0
    for axis_at, blocks in pieces:
        steps = jax.random.uniform(jax.random.fold_in(jax.random.fold_in(stream_key, 6), axis_at), (blocks,), jnp.float32, low / len(pieces), top_value / len(pieces))
        gain = gain * jnp.repeat(jnp.exp(steps), extent[axis_at] // blocks).reshape((-1,) + (1,) * (len(extent) - 1 - axis_at))
    return gain


def bell_draw(own_key, extent, width, reach, cuts=(), kind=jnp.bfloat16):
    array = jax.random.normal(own_key, extent, jnp.float32) * width
    if len(cuts) > 0:
        array = steps_of(own_key, extent, cuts, -0.22, 0.18) * array
    return jnp.clip(array, min=-reach, max=reach).astype(kind)


def setup_inputs(seed: int = 0) -> dict:
    key_of = jax.random.split(jax.random.key(seed), 5)
    tokens = draw_tokens(jax.random.fold_in(key_of[4], 71), 0)
    gate_weight = bell_draw(key_of[1], (D, FF), D ** -0.5, 0.046875, ((0, 16), (1, 16)))
    up_weight = bell_draw(key_of[2], (D, FF), D ** -0.5, 0.046875, ((0, 16), (1, 16)))
    down_weight = bell_draw(key_of[3], (FF, D), FF ** -0.5, 0.0390625, ((0, 16), (1, 16)))
    return {"tokens": tokens, "gate_weight": gate_weight, "up_weight": up_weight, "down_weight": down_weight}


def reference(tokens, gate_weight, up_weight, down_weight):
    gate = jnp.dot(tokens, gate_weight, preferred_element_type=jnp.float32)
    up = jnp.dot(tokens, up_weight, preferred_element_type=jnp.float32)
    hidden = (jax.nn.silu(gate) * up).astype(jnp.bfloat16)
    total = tokens.astype(jnp.float32) + jnp.dot(hidden, down_weight, preferred_element_type=jnp.float32)
    return total.astype(jnp.bfloat16)
```

```python
import jax
import jax.numpy as jnp
from jax import lax
from jax.experimental import pallas as pl
from jax.experimental.pallas import tpu as pltpu
from jax.sharding import PartitionSpec as P

MESH = pl.DeviceIdType.MESH
BF16 = jnp.bfloat16
F32 = jnp.float32

ROWS = 32
PIECE = 16
LANES = 128
TILES = 13
FF = TILES * LANES
HALF = 512
GROUPS = ((0, 7), (7, 13))
CUT = 7 * LANES
N_SEMS = 160


def block_kernel(
    tokens, wg, wu, wd, out,
    w_gu, w_dn, tok, acc, xs, xr, sg, su, rg, gys, gyr, g_own, ru, us, u_own, rx, hid,
    o_f, sa1, ra1, sa2, ra2, sa3, ra3, sa4, ra4, ya_s, ya_r, yb_s, yb_r, b_f,
    sb1, rb1, sb2, rb2, sb3, rb3, sb4, rb4, w_sem, d_sem, t_sem, ss, rs,
):
    gx, gy = lax.axis_index("gx"), lax.axis_index("gy")
    x, yl, c = lax.div(gx, 4), lax.rem(lax.div(gx, 2), 2), lax.rem(gx, 2)
    z, yh = lax.div(gy, 2), lax.rem(gy, 2)

    def xat(k):
        return lax.rem(x + k + 4, 4)

    def zat(k):
        return lax.rem(z + k + 8, 8)

    def to_x(k):
        return (xat(k) * 4 + yl * 2 + c, gy)

    def to_z(k):
        return (gx, zat(k) * 2 + yh)

    to_yl = (x * 4 + (1 - yl) * 2 + c, gy)
    to_core = (x * 4 + yl * 2 + (1 - c), gy)
    to_yh = (gx, z * 2 + (1 - yh))

    t_copy = pltpu.make_async_copy(tokens, tok.at[yh], t_sem)
    t_copy.start()

    def w_copy(g, i):
        lo, hi = GROUPS[g]
        n = (hi - lo) * LANES
        return pltpu.make_async_copy(
            (wg, wu)[i].at[:, pl.ds(lo * LANES, n)],
            w_gu.at[:, pl.ds(2 * lo * LANES + i * n, n)],
            w_sem.at[g, i],
        )

    d_copy = pltpu.make_async_copy(wd, w_dn, d_sem)

    barrier = pltpu.get_barrier_semaphore()
    peers = [to_z(1), to_z(-1), to_yh, to_z(2), to_z(-2), to_x(1), to_x(3), to_x(2), to_yl, to_core]
    for p in peers:
        pl.semaphore_signal(barrier, inc=1, device_id=p, device_id_type=MESH)
    t_copy.wait()
    pl.semaphore_wait(barrier, len(peers))

    sent = []
    count = [0]

    def send(src, dst, device):
        i = count[0]
        count[0] += 1
        cp = pltpu.make_async_remote_copy(
            src_ref=src, dst_ref=dst, send_sem=ss.at[i], recv_sem=rs.at[i],
            device_id=device, device_id_type=MESH,
        )
        cp.start()
        sent.append(cp)
        return cp


    def pass_on(slot):
        return send(tok.at[slot], tok.at[slot], to_yh)

    def near_two(a):
        return send(tok.at[a], tok.at[6 + a], to_z(4 * a - 2))

    def far_two(a):
        return send(tok.at[a], tok.at[8 + a], to_z(2 - 4 * a))

    def forward_near(a):
        rows = pl.ds(pl.multiple_of((1 - a) * PIECE, PIECE), PIECE)
        return [
            send(tok.at[6 + a], tok.at[10 + 3 * a], to_z(2 * a - 1)),
            send(tok.at[6 + a, rows], tok.at[14 + a, rows], to_z(4 * a - 2)),
        ]

    def forward_far(a):
        rows = pl.ds(pl.multiple_of(a * PIECE, PIECE), PIECE)
        return [
            send(tok.at[8 + a], tok.at[12 - a], to_z(1 - 2 * a)),
            send(tok.at[8 + a, rows], tok.at[14 + a, rows], to_z(2 - 4 * a)),
        ]

    yo = 1 - yh
    y_0 = pass_on(yh)
    z_r = send(tok.at[yh], tok.at[4 + yh], to_z(1))
    z_l = send(tok.at[yh], tok.at[2 + yh], to_z(-1))
    z_n = near_two(yh)
    for g in range(2):
        for i in range(2):
            w_copy(g, i).start()
    z_f = far_two(yh)
    y_0.wait_recv()
    z_no = near_two(yo)
    z_fo = far_two(yo)
    z_r.wait_recv()
    y_r = pass_on(4 + yh)
    z_l.wait_recv()
    y_l = pass_on(2 + yh)
    z_n.wait_recv()
    z_34 = forward_near(yh)
    z_f.wait_recv()
    z_34 += forward_far(yh)
    y_n = [y_r, y_l, z_no]

    def far_tokens():
        z = forward_near(yo)
        z_fo.wait_recv()
        return z_34 + z + forward_far(yo)

    def products(k, waits):
        cps = []
        for cp in waits:
            cp.wait_recv()
        rows = tok[pl.ds(8 * k, 8)].reshape(256, 1024)
        for g, (lo, hi) in enumerate(GROUPS):
            if k == 0:
                for i in range(2):
                    w_copy(g, i).wait()
            n = (hi - lo) * 256
            acc[g, :, :, pl.ds(0, n)] = jnp.dot(
                rows, w_gu[:, lo * 256 : hi * 256], preferred_element_type=F32
            ).reshape(2, 128, n)
            xs[k, g, :, pl.ds(0, n)] = acc[g, 1 - c, :, pl.ds(0, n)].astype(BF16)
            cps.append(
                send(xs.at[k, g, :, pl.ds(0, n)], xr.at[k, g, :, pl.ds(0, n)], to_core)
            )
        return cps

    def pair_sums(k, cps):
        gate_x, up_y = [], []
        for g, (lo, hi) in enumerate(GROUPS):
            cps[g].wait_recv()

            def add(t, carry):
                def total(i):
                    start = (t - lo + i * (hi - lo)) * LANES
                    cols = pl.ds(pl.multiple_of(start, LANES), LANES)
                    v = acc[g, c, :, cols] + xr[k, g, :, cols].astype(F32)
                    return v.reshape(4, 2, PIECE, LANES).astype(BF16)

                sg[k, t] = total(0)
                su[k, t] = total(1)
                return carry

            lax.fori_loop(lo, hi, add, 0)
            ts = pl.ds(lo, hi - lo)
            up_y.append(send(su.at[k, ts, :, 1 - yl], ru.at[k, ts], to_yl))
            gate_x.append(
                [send(sg.at[k, ts, xat(j)], rg.at[k, j - 1, ts], to_x(j)) for j in (1, 3, 2)]
            )
        return gate_x, up_y

    def chip_sums(k, gate_x, up_y):
        gate_y, up_x = [], []
        for g, (lo, hi) in enumerate(GROUPS):
            ts = pl.ds(lo, hi - lo)
            up_y[g].wait_recv()

            def add_up(t, carry):
                us[k, t] = (su[k, t, :, yl].astype(F32) + ru[k, t].astype(F32)).astype(BF16)
                u_own[k, t] = su[k, t, x, yl].astype(F32) + ru[k, t, x].astype(F32)
                return carry

            lax.fori_loop(lo, hi, add_up, 0)
            up_x.append(
                [send(us.at[k, ts, xat(j)], rx.at[k, j - 1, ts], to_x(j)) for j in (1, 3, 2)]
            )
            for cp in gate_x[g]:
                cp.wait_recv()

            def add_gate(t, carry):
                def total(y):
                    return (
                        sg[k, t, x, y].astype(F32) + rg[k, 0, t, y].astype(F32)
                        + rg[k, 1, t, y].astype(F32) + rg[k, 2, t, y].astype(F32)
                    )

                gys[k, t] = total(1 - yl).astype(BF16)
                g_own[k, t] = total(yl)
                return carry

            lax.fori_loop(lo, hi, add_gate, 0)
            gate_y.append(send(gys.at[k, ts], gyr.at[k, ts], to_yl))
        return gate_y, up_x

    h0, h1 = pl.ds(0, CUT), pl.ds(CUT, FF - CUT)
    every = slice(None)

    def activate(k, g, gate_y, up_x):
        lo, hi = GROUPS[g]
        gate_y[g].wait_recv()
        for cp in up_x[g]:
            cp.wait_recv()
        for t in range(lo, hi):
            gate = g_own[k, t] + gyr[k, t].astype(F32)
            up = (
                u_own[k, t] + rx[k, 0, t].astype(F32) + rx[k, 1, t].astype(F32)
                + rx[k, 2, t].astype(F32)
            )
            h = gate / (1.0 + jnp.exp(-gate)) * up
            hid[k, c, x, yl, :, pl.ds(t * LANES, LANES)] = h.astype(BF16)

    def share(index, device):
        return send(hid.at[index], hid.at[index], device)

    def spread(k, gate_y, up_x):
        activate(k, 0, gate_y, up_x)
        mine = (k, c, x, yl, every, h0)
        p_y = [share(mine, to_yl)]
        p_x = [share(mine, to_x(j)) for j in (1, 3, 2)]
        p_c = [share(mine, to_core)]
        activate(k, 1, gate_y, up_x)
        q_y = share((k, c, x, yl, every, h1), to_yl)
        return p_x, p_y, p_c, q_y

    def spread_on(k, p_x, p_y, p_c, q_y):
        q_y.wait_recv()
        both = (k, c, x, every, every, h1)
        q_x = [share(both, to_x(j)) for j in (1, 3, 2)]
        p_c.append(share(both, to_core))
        for i, j in enumerate((1, 3, 2)):
            p_x[i].wait_recv()
            piece = (k, c, xat(-j), yl, every, h0)
            p_y.append(share(piece, to_yl))
            p_c.append(share(piece, to_core))
        return p_y, q_x, p_c

    def spread_last(k, p_y, q_x, p_c):
        for i, j in enumerate((0, 1, 3, 2)):
            p_y[i].wait_recv()
            p_c.append(share((k, c, xat(-j), 1 - yl, every, h0), to_core))
        for i, j in enumerate((1, 3, 2)):
            q_x[i].wait_recv()
            p_c.append(share((k, c, xat(-j), every, every, h1), to_core))
        return p_c

    ca, cb = pl.ds(0, HALF), pl.ds(HALF, HALF)

    def down(k, cols):
        o_f[pl.ds(4 * k, 4), :, :, cols] = jnp.dot(
            hid[k].reshape(256, FF), w_dn[:, cols], preferred_element_type=F32
        ).reshape(4, 2, ROWS, HALF)

    def part(slot, cols):
        return o_f[slot // 2, slot % 2, :, cols]

    def put(buf, value, device, dst):
        buf[...] = value.astype(BF16)
        return send(buf, dst, device)

    def y_first(k):
        return put(yb_s.at[k], o_f[pl.ds(4 * k, 4), 1 - yh, :, cb], to_yh, yb_r.at[k])

    def y_add(k, cp):
        cp.wait_recv()
        ks = pl.ds(4 * k, 4)
        b_f[ks] = o_f[ks, yh, :, cb] + yb_r[k].astype(F32)

    for cp in y_n:
        cp.wait_recv()
    y_f = far_tokens()
    core_0 = products(0, [])
    d_copy.start()
    gate_x0, up_y0 = pair_sums(0, core_0)
    core_1 = products(1, y_f)
    gate_y0, up_x0 = chip_sums(0, gate_x0, up_y0)
    gate_x1, up_y1 = pair_sums(1, core_1)
    spread_0 = spread(0, gate_y0, up_x0)
    gate_y1, up_x1 = chip_sums(1, gate_x1, up_y1)
    on_0 = spread_on(0, *spread_0)
    spread_1 = spread(1, gate_y1, up_x1)
    p_c0 = spread_last(0, *on_0)
    d_copy.wait()
    on_1 = spread_on(1, *spread_1)
    for cp in p_c0:
        cp.wait_recv()
    down(0, ca)
    a_1r = put(sa1.at[0], o_f[1, :, :, ca], to_z(1), ra1.at[0])
    a_1l = put(sa1.at[1], o_f[2, :, :, ca], to_z(-1), ra1.at[1])
    p_c1 = spread_last(1, *on_1)
    down(0, cb)
    b_y0 = y_first(0)
    for cp in p_c1:
        cp.wait_recv()
    down(1, cb)
    b_y1 = y_first(1)
    down(1, ca)
    a_3r = put(sa3.at[0], o_f[5, :, :, ca], to_z(1), ra3.at[0])
    a_3l = put(sa3.at[1], o_f[6, :, :, ca], to_z(-1), ra3.at[1])
    a_4r = put(sa4.at[0], part(14, ca), to_z(2), ra4.at[0])
    a_4l = put(sa4.at[1], part(15, ca), to_z(-2), ra4.at[1])
    y_add(0, b_y0)
    b_1r = put(sb1.at[0], b_f[1], to_z(1), rb1.at[0])
    b_1l = put(sb1.at[1], b_f[2], to_z(-1), rb1.at[1])
    y_add(1, b_y1)
    top, low = pl.ds(0, PIECE), pl.ds(PIECE, PIECE)
    b_3r = put(sb3.at[0], b_f[5], to_z(1), rb3.at[0])
    b_3l = put(sb3.at[1], b_f[6], to_z(-1), rb3.at[1])
    b_4r = put(sb4.at[0], b_f[7, top], to_z(2), rb4.at[0])
    b_4l = put(sb4.at[1], b_f[7, low], to_z(-2), rb4.at[1])
    a_3r.wait_recv()
    a_4r.wait_recv()
    sa2[0, 0] = (part(6, ca) + ra3[0, 0].astype(F32) + ra4[0].astype(F32)).astype(BF16)
    sa2[0, 1] = (part(9, ca) + ra3[0, 1].astype(F32)).astype(BF16)
    a_2r = send(sa2.at[0], ra2.at[0], to_z(2))
    a_3l.wait_recv()
    a_4l.wait_recv()
    sa2[1, 0] = (part(8, ca) + ra3[1, 0].astype(F32)).astype(BF16)
    sa2[1, 1] = (part(7, ca) + ra3[1, 1].astype(F32) + ra4[1].astype(F32)).astype(BF16)
    a_2l = send(sa2.at[1], ra2.at[1], to_z(-2))
    b_3r.wait_recv()
    b_4r.wait_recv()
    two_r, two_l = 3 + yh, 4 - yh
    sb2[0, top] = (
        b_f[two_r, top] + rb3[0, top].astype(F32) + rb4[0].astype(F32)
    ).astype(BF16)
    sb2[0, low] = (b_f[two_r, low] + rb3[0, low].astype(F32)).astype(BF16)
    b_2r = send(sb2.at[0], rb2.at[0], to_z(2))
    b_3l.wait_recv()
    b_4l.wait_recv()
    sb2[1, top] = (b_f[two_l, top] + rb3[1, top].astype(F32)).astype(BF16)
    sb2[1, low] = (
        b_f[two_l, low] + rb3[1, low].astype(F32) + rb4[1].astype(F32)
    ).astype(BF16)
    b_2l = send(sb2.at[1], rb2.at[1], to_z(-2))
    for cp in (a_1r, a_1l, a_2r, a_2l):
        cp.wait_recv()

    def a_total(y):
        total = o_f[0, y, :, ca]
        for r in (ra1, ra2):
            total = total + r[0, y].astype(F32) + r[1, y].astype(F32)
        return total

    a_y = put(ya_s, a_total(1 - yh), to_yh, ya_r)
    mine_a = tok[yh, :, ca].astype(F32) + a_total(yh)
    for cp in (b_1r, b_1l, b_2r, b_2l):
        cp.wait_recv()
    mine_b = b_f[0]
    for r in (rb1, rb2):
        mine_b = mine_b + r[0].astype(F32) + r[1].astype(F32)
    out[:, cb] = (tok[yh, :, cb].astype(F32) + mine_b).astype(BF16)
    a_y.wait_recv()
    out[:, ca] = (mine_a + ya_r[...].astype(F32)).astype(BF16)

    for cp in sent:
        cp.wait_send()


def on_device(tokens, gate_weight, up_weight, down_weight):
    vmem = pl.BlockSpec(memory_space=pltpu.VMEM)
    hbm = pl.BlockSpec(memory_space=pltpu.HBM)
    tile = (PIECE, LANES)

    def buf(*shape, dtype=BF16):
        return pltpu.VMEM(shape, dtype)

    return pl.pallas_call(
        block_kernel,
        out_shape=jax.ShapeDtypeStruct(tokens.shape, BF16),
        in_specs=[hbm] * 4,
        out_specs=vmem,
        scratch_shapes=[
            buf(1024, 2 * FF),
            buf(FF, 1024),
            buf(16, ROWS, 1024),
            buf(2, 2, 128, 1792, dtype=F32),
            buf(2, 2, 128, 1792),
            buf(2, 2, 128, 1792),
            buf(2, TILES, 4, 2, *tile),
            buf(2, TILES, 4, 2, *tile),
            buf(2, 3, TILES, 2, *tile),
            buf(2, TILES, *tile),
            buf(2, TILES, *tile),
            buf(2, TILES, *tile, dtype=F32),
            buf(2, TILES, 4, *tile),
            buf(2, TILES, 4, *tile),
            buf(2, TILES, *tile, dtype=F32),
            buf(2, 3, TILES, *tile),
            buf(2, 2, 4, 2, PIECE, FF),
            buf(8, 2, ROWS, 1024, dtype=F32),
            buf(2, 2, ROWS, HALF),
            buf(2, 2, ROWS, HALF),
            buf(2, 2, ROWS, HALF),
            buf(2, 2, ROWS, HALF),
            buf(2, 2, ROWS, HALF),
            buf(2, 2, ROWS, HALF),
            buf(2, ROWS, HALF),
            buf(2, ROWS, HALF),
            buf(ROWS, HALF),
            buf(ROWS, HALF),
            buf(2, 4, ROWS, HALF),
            buf(2, 4, ROWS, HALF),
            buf(8, ROWS, HALF, dtype=F32),
            buf(2, ROWS, HALF),
            buf(2, ROWS, HALF),
            buf(2, ROWS, HALF),
            buf(2, ROWS, HALF),
            buf(2, ROWS, HALF),
            buf(2, ROWS, HALF),
            buf(2, PIECE, HALF),
            buf(2, PIECE, HALF),
            pltpu.SemaphoreType.DMA((2, 2)),
            pltpu.SemaphoreType.DMA,
            pltpu.SemaphoreType.DMA,
            pltpu.SemaphoreType.DMA((N_SEMS,)),
            pltpu.SemaphoreType.DMA((N_SEMS,)),
        ],
        compiler_params=pltpu.CompilerParams(
            collective_id=0, has_side_effects=True, vmem_limit_bytes=52 * 2**20
        ),
        cost_estimate=pl.CostEstimate(
            flops=5_300_000_000, bytes_accessed=10_500_000, transcendentals=60_000
        ),
    )(tokens, gate_weight, up_weight, down_weight)


def solution(mesh):
    in_specs = (P("gy", "gx"), P("gx", "gy"), P("gx", "gy"), P("gy", "gx"))
    return jax.shard_map(
        on_device, mesh=mesh, in_specs=in_specs, out_specs=P("gy", "gx"), check_vma=False
    )
```
